32 devices in a mesh: sector: 4 (over z), mode: 8 (over y, x, core).
Axes of the slice: x: 2, y: 2, z: 4, core: 2. Of those that a mesh axis runs over, the one named last changes fastest.
Arguments:
- modes: bfloat16 [256, 3, 16, 80, 128], P('mode', None, 'sector'), may hold values from -0.21875 to 0.21875
- thickness: float32 [16, 80, 128], P('sector'), may hold values from -6 to 6
- stiff_taps: float32 [27], replicated, may hold values from -1.25 to 1.25
- mass_taps: float32 [27], replicated, may hold values from 0.02 to 0.2
- eigenvalues: float32 [256], P('mode'), may hold values from 0.5 to 2
Outputs:
- sensitivity: float32 [256, 256], P('sector', 'mode')
The draws below stay inside these ranges and needn't reach their ends.
All inputs are finite; a program needn't handle non-finite values.
Results may differ from the reference program's by a relative error of at most 0.0029.
Values may be sent and summed in bfloat16 or wider, within the bound.
No kernel may reach another device: no remote copies, remote signals or barrier semaphores. Data moves between devices by JAX's collectives and lax.ppermute only.
A program may use at most 128 MiB of HBM per device.

```python
import math
import jax
import jax.numpy as jnp
from jax import lax

MODES = 256
COMP = 3
NY = 80
NZ = 128
NX = 16


def levels(rng, dims, split, smallest, top_value):
    def one(position, shards_of):
        steps = jax.random.uniform(jax.random.fold_in(jax.random.fold_in(rng, 6), position), (shards_of,), jnp.float32, smallest / len(split), top_value / len(split))
        return jnp.repeat(jnp.exp(steps), dims[position] // shards_of).reshape((-1,) + (1,) * (len(dims) - position - 1))

    loudness = one(*split[0])
    for cut in split[1:]:
        loudness = loudness * one(*cut)
    return loudness


def bell_draw(key, dims, scale, reach, pieces=(), dtype=jnp.bfloat16):
    array = scale * jax.random.normal(key, dims, jnp.float32)
    if pieces:
        array = array * levels(key, dims, pieces, -0.22, 0.18)
    return jnp.clip(array, -reach, reach).astype(dtype)


def setup_inputs(seed: int = 0) -> dict:
    keys = jax.random.split(jax.random.key(seed), 6)
    return {
        "modes": bell_draw(keys[0], (MODES, COMP, NX, NY, NZ), ((COMP * NX * NY * NZ) ** -0.25), 0.21875, ((0, 8), (2, 4))),
        "thickness": bell_draw(keys[1], (NX, NY, NZ), 1.0, 6.0, ((0, 4),), jnp.float32),
        "stiff_taps": bell_draw(keys[2], (27,), 0.2, 1.25, (), jnp.float32),
        "mass_taps": jnp.clip(jnp.exp(jax.random.uniform(keys[3], (27,), jnp.float32, math.log(0.02), math.log(0.2))), 0.02, 0.2),
        "eigenvalues": jnp.clip(jnp.exp(math.log(2.0) - 1.3862944 * jax.random.uniform(keys[4], (MODES,), jnp.float32) ** levels(keys[4], (MODES,), ((0, 8),), -0.2, 0.2)), 0.5, 2.0),
    }


def load_block(block, lams, padded_thick, stiff_taps, mass_taps):
    field = jnp.pad(block.astype(jnp.float32), ((0, 0), (0, 0), (1, 1), (1, 1), (1, 1)))
    sx = field.shape[2] - 2
    sy = field.shape[3] - 2
    sz = field.shape[4] - 2
    centre = padded_thick[1:1 + sx, 1:1 + sy, 1:1 + sz]
    stiff_acc = jnp.zeros(block.shape, jnp.float32)
    mass_acc = jnp.zeros(block.shape, jnp.float32)
    for aoff in range(3):
        for boff in range(3):
            for doff in range(3):
                index = 9 * aoff + 3 * boff + doff
                coeff = 0.5 * (centre + padded_thick[aoff:aoff + sx, boff:boff + sy, doff:doff + sz])
                moved = coeff * field[:, :, aoff:aoff + sx, boff:boff + sy, doff:doff + sz]
                stiff_acc = stiff_acc + stiff_taps[index] * moved
                mass_acc = mass_acc + mass_taps[index] * moved
    loaded = stiff_acc - lams[:, None, None, None, None] * mass_acc
    return loaded.astype(jnp.bfloat16)


def reference(modes, thickness, stiff_taps, mass_taps, eigenvalues):
    padded_thick = jnp.pad(thickness, 1)
    count = modes.shape[0] // 16
    blocks = modes.reshape((count, 16) + modes.shape[1:])
    lam_blocks = eigenvalues.reshape(count, 16)
    loaded = lax.map(lambda pair: load_block(pair[0], pair[1], padded_thick, stiff_taps, mass_taps), (blocks, lam_blocks))
    loaded = loaded.reshape(modes.shape[0], -1)
    return jnp.dot(modes.reshape(modes.shape[0], -1), loaded.T, preferred_element_type=jnp.float32)
```

```python
import functools

import jax
import jax.numpy as jnp
from jax import lax
from jax.experimental import pallas as pl
from jax.experimental.pallas import tpu as pltpu
from jax.sharding import PartitionSpec as P

VMEM_BYTES = 56 * 1024 * 1024
AB = [(a, b) for a in range(3) for b in range(3)]


def chunk_rows(total):
    sizes = [4, 6, 6, 4, 2]
    if sum(sizes) == total:
        return sizes
    sizes = []
    while total > 6:
        sizes.append(4)
        total -= 4
    return sizes + [total]


def pack_kernel(height, parts, chunks, me_ref, in_ref, *rest):
    outs, scr = rest[:-1], rest[-1]
    comps, size_y = in_ref.shape[1], in_ref.shape[3]
    first = chunks[0][0]
    last = chunks[-1][1]
    me = me_ref[0]
    for c in range(comps):
        for start in range(0, size_y, 16):
            wanted = [
                (p, e - first, height * p - 1 + e)
                for p in range(parts)
                for e in range(first, last)
                if start <= height * p - 1 + e < start + 16
            ]
            if not wanted:
                continue
            turned = jnp.swapaxes(in_ref[:, c, 0, start : start + 16, :], 0, 1)
            for p, e, y in wanted:
                scr[p, e, c] = turned[y - start]
        for p in range(parts):
            for e in range(first, last):
                if not 0 <= height * p - 1 + e < size_y:
                    scr[p, e - first, c] = jnp.zeros(scr.shape[3:], scr.dtype)
    for r, (lo, hi) in enumerate(chunks):
        for k in range(parts):
            outs[r * parts + k][0] = scr[me ^ k, lo - first : hi - first]


def pack(modes, me, height, parts, chunks):
    local, comps, planes, size_y, size_z = modes.shape
    shapes = [
        jax.ShapeDtypeStruct((planes, hi - lo, comps, local, size_z), modes.dtype)
        for lo, hi in chunks
        for _ in range(parts)
    ]
    count = chunks[-1][1] - chunks[0][0]
    outs = pl.pallas_call(
        functools.partial(pack_kernel, height, parts, chunks),
        grid=(planes,),
        in_specs=[
            pl.BlockSpec(memory_space=pltpu.SMEM),
            pl.BlockSpec((local, comps, 1, size_y, size_z), lambda x: (0, 0, x, 0, 0)),
        ],
        out_specs=[pl.BlockSpec((1,) + s.shape[1:], lambda x: (x, 0, 0, 0, 0)) for s in shapes],
        out_shape=shapes,
        scratch_shapes=[pltpu.VMEM((parts, count, comps, local, size_z), modes.dtype)],
        compiler_params=pltpu.CompilerParams(vmem_limit_bytes=VMEM_BYTES),
        name="pack",
        cost_estimate=pl.CostEstimate(flops=0, bytes_accessed=2 * modes.size * 2, transcendentals=0),
    )(me, modes)
    return [outs[r * parts : (r + 1) * parts] for r in range(len(chunks))]


def load_kernel(prev_rows, rows, own, *refs):
    if prev_rows:
        (u_ref, lam_ref, s_ref, f_ref, lo_ref, hi_ref, e_ref, fp_ref, lop_ref, hip_ref, ep_ref,
         out_ref, win, other, g_ref, l_ref, sems) = refs
    else:
        (u_ref, lam_ref, f_ref, lo_ref, hi_ref, e_ref,
         out_ref, win, other, g_ref, l_ref, sems) = refs
    planes = f_ref.shape[0]
    size_z = f_ref.shape[-1]
    comps = f_ref.shape[2] // own
    keep = 2 if prev_rows else 0
    done = rows - 2 + keep
    copies = [
        (f_ref, win.at[1 : 1 + planes, keep : keep + rows]),
        (lo_ref, win.at[0, keep : keep + rows]),
        (hi_ref, win.at[planes + 1, keep : keep + rows]),
    ]
    if prev_rows:
        copies += [
            (fp_ref.at[:, prev_rows - 2 : prev_rows], win.at[1 : 1 + planes, 0:2]),
            (lop_ref.at[prev_rows - 2 : prev_rows], win.at[0, 0:2]),
            (hip_ref.at[prev_rows - 2 : prev_rows], win.at[planes + 1, 0:2]),
            (e_ref.at[:, 0 : rows - 1], other.at[:, 1:rows]),
            (ep_ref.at[:, prev_rows - 1 : prev_rows], other.at[:, 0:1]),
        ]
    else:
        copies += [(e_ref.at[:, 1 : rows - 1], other)]
    started = [pltpu.make_async_copy(src, dst, sems.at[n]) for n, (src, dst) in enumerate(copies)]
    for copy in started:
        copy.start()
    if prev_rows:
        out_ref[...] = s_ref[...]
    else:
        out_ref[...] = jnp.zeros_like(out_ref)
    for copy in started:
        copy.wait()

    gap = lax.broadcasted_iota(jnp.int32, (size_z, size_z), 0) - lax.broadcasted_iota(
        jnp.int32, (size_z, size_z), 1
    )
    diag = [gap == d - 1 for d in range(3)]

    def row(y, _):
        for x in range(planes):
            u = u_ref[y, x]
            high = u.astype(jnp.bfloat16).astype(jnp.float32)
            low = u - high
            for ab in range(9):
                for half, part in enumerate((high, low)):
                    for kind in range(2):
                        base = 27 * kind + 3 * ab
                        band = jnp.zeros((size_z, size_z), jnp.float32)
                        for d in range(3):
                            band = jnp.where(diag[d], part[base + d : base + d + 1], band)
                        g_ref[
                            (2 * ab + half) * size_z : (2 * ab + half + 1) * size_z,
                            kind * size_z : (kind + 1) * size_z,
                        ] = band.astype(jnp.bfloat16)
            around = []
            for a, b in AB:
                near = win[x + a, y + b]
                around += [near, near]
            images = jnp.dot(
                jnp.concatenate(around, axis=1), g_ref[...], preferred_element_type=jnp.float32
            )
            for c in range(comps):
                image = images[c * own : (c + 1) * own]
                l_ref[:, (x * comps + c) * size_z : (x * comps + c + 1) * size_z] = (
                    image[:, :size_z] - lam_ref[...] * image[:, size_z:]
                ).astype(jnp.bfloat16)
        cells = [(x, c) for x in range(planes) for c in range(comps)]
        mine = jnp.concatenate([win[x + 1, y + 1, c * own : (c + 1) * own] for x, c in cells], axis=1)
        theirs = jnp.concatenate([other[x, y, c * own : (c + 1) * own] for x, c in cells], axis=1)
        out_ref[...] += lax.dot_general(
            jnp.concatenate([mine, theirs], axis=0),
            l_ref[...],
            (((1,), (1,)), ((), ())),
            preferred_element_type=jnp.float32,
        )
        return 0

    lax.fori_loop(0, done, row, 0)


def load(u, lam, sums, now, before, own):
    rows = now[0].shape[1]
    planes, _, width, size_z = now[0].shape
    prev_rows = before[0].shape[1] if before else 0
    done = rows if before else rows - 2
    vmem = pl.BlockSpec(memory_space=pltpu.VMEM)
    hbm = pl.BlockSpec(memory_space=pl.ANY)
    args = [u, lam] + ([sums] if before else []) + list(now) + (list(before) if before else [])
    specs = [vmem] * (3 if before else 2) + [hbm] * (8 if before else 4)
    out = jax.ShapeDtypeStruct((2 * own, own), jnp.float32)
    taps = 2 * 9 * size_z
    return pl.pallas_call(
        functools.partial(load_kernel, prev_rows, rows, own),
        in_specs=specs,
        out_specs=vmem,
        out_shape=out,
        scratch_shapes=[
            pltpu.VMEM((planes + 2, done + 2, width, size_z), jnp.bfloat16),
            pltpu.VMEM((planes, done, width, size_z), jnp.bfloat16),
            pltpu.VMEM((taps, 2 * size_z), jnp.bfloat16),
            pltpu.VMEM((own, planes * width // own * size_z), jnp.bfloat16),
            pltpu.SemaphoreType.DMA((8,)),
        ],
        compiler_params=pltpu.CompilerParams(vmem_limit_bytes=VMEM_BYTES),
        name="load",
        cost_estimate=pl.CostEstimate(
            flops=2 * done * planes * width * taps * 2 * size_z,
            bytes_accessed=4 * done * planes * width * size_z,
            transcendentals=0,
        ),
    )(*args)


def arrange_kernel(parts, local, pos_ref, s_ref, *outs):
    *outs, rows_ref = outs
    me, mine = pos_ref[0], pos_ref[1]
    own = parts * local
    for h in range(2):
        for k in range(parts):
            slot = (me ^ k) * 2 + (mine ^ h)
            rows_ref[slot] = s_ref[h * own + k * local : h * own + (k + 1) * local]
    whole = rows_ref[...].reshape(2 * own, own)
    for k, out in enumerate(outs):
        rows, lanes = out.shape
        strips = lanes // local
        out[...] = jnp.concatenate(
            [whole[n * rows : (n + 1) * rows, k * local : (k + 1) * local] for n in range(strips)], axis=1
        )


def arrange(pos, sums, parts, local, sectors):
    total, own = sums.shape
    rows = total // sectors
    return pl.pallas_call(
        functools.partial(arrange_kernel, parts, local),
        in_specs=[pl.BlockSpec(memory_space=pltpu.SMEM), pl.BlockSpec(memory_space=pltpu.VMEM)],
        out_specs=[pl.BlockSpec(memory_space=pltpu.VMEM)] * parts,
        out_shape=[jax.ShapeDtypeStruct((rows, sectors * local), jnp.float32)] * parts,
        scratch_shapes=[pltpu.VMEM((2 * parts, local, own), jnp.float32)],
        name="arrange",
    )(pos, sums)


def on_device(modes, thickness, stiff_taps, mass_taps, eigenvalues):
    local, comps, planes, size_y, size_z = modes.shape
    sectors, groups = lax.axis_size("sector"), lax.axis_size("mode")
    parts = groups // 2
    height = size_y // parts
    own = parts * local
    index = lax.axis_index("mode")
    me, mine = index // 2, index % 2

    def other_part(value, k):
        return lax.ppermute(value, "mode", [(i, i ^ (2 * k)) for i in range(groups)])

    def other_half(value):
        return lax.ppermute(value, "mode", [(i, i ^ 1) for i in range(groups)])

    def from_below(value):
        return lax.ppermute(value, "sector", [(i, i + 1) for i in range(sectors - 1)])

    def from_above(value):
        return lax.ppermute(value, "sector", [(i + 1, i) for i in range(sectors - 1)])

    bounds, at = [], 0
    for size in chunk_rows(height + 2):
        bounds.append((at, at + size))
        at += size
    me_word = me.astype(jnp.int32).reshape(1)
    packed = pack(modes, me_word, height, parts, bounds[:1])
    packed += pack(modes, me_word, height, parts, bounds[1:])

    thick = jnp.concatenate([from_below(thickness[-1:]), thickness, from_above(thickness[:1])], axis=0)
    thick = jnp.pad(thick, ((0, 0), (1, 1), (1, 1)))
    thick = lax.dynamic_slice_in_dim(thick, me * height, height + 2, axis=1)
    centre = thick[1 : 1 + planes, 1 : 1 + height, 1 : 1 + size_z]
    coeffs = jnp.stack(
        [
            0.5 * (centre + thick[a : a + planes, b : b + height, d : d + size_z])
            for a in range(3)
            for b in range(3)
            for d in range(3)
        ],
        axis=2,
    )
    coeffs = jnp.concatenate(
        [coeffs * stiff_taps[:, None], coeffs * mass_taps[:, None]], axis=2
    ).transpose(1, 0, 2, 3)

    lams = jnp.concatenate(
        [eigenvalues] + [other_part(eigenvalues, k) for k in range(1, parts)], axis=0
    )
    lams = jnp.broadcast_to(lams[:, None], (own, size_z))

    sums, before, at = None, None, 0
    for (lo, hi), blocks in zip(bounds, packed):
        got = [blocks[0]] + [other_part(blocks[k], k) for k in range(1, parts)]
        field = jnp.concatenate(got, axis=3).reshape(planes, hi - lo, comps * own, size_z)
        now = (field, from_below(field[-1]), from_above(field[0]), other_half(field))
        done = hi - lo - (0 if before else 2)
        sums = load(coeffs[at : at + done], lams, sums, now, before, own)
        at += done
        before = now

    pos = jnp.stack([me, mine]).astype(jnp.int32)
    strips = arrange(pos, sums, parts, local, sectors)
    total = strips[0]
    for k in range(1, parts):
        total = total + other_part(strips[k], k)
    summed = total
    for step in range(1, sectors):
        summed = summed + lax.ppermute(
            total, "sector", [(i, (i + step) % sectors) for i in range(sectors)]
        )
    return lax.dynamic_slice_in_dim(summed, lax.axis_index("sector") * local, local, axis=1)


def solution(mesh):
    in_specs = (P("mode", None, "sector", None, None), P("sector", None, None), P(), P(), P("mode"))
    out_specs = P("sector", "mode")
    return jax.shard_map(
        on_device, mesh=mesh, in_specs=in_specs, out_specs=out_specs, check_vma=False
    )
```

```python
import functools

import jax
import jax.numpy as jnp
from jax import lax
from jax.experimental import pallas as pl
from jax.experimental.pallas import tpu as pltpu
from jax.sharding import PartitionSpec as P

VMEM_BYTES = 56 * 1024 * 1024
AB = [(a, b) for a in range(3) for b in range(3)]


def chunk_rows(total):
    sizes = [4, 6, 6, 4, 2]
    if sum(sizes) == total:
        return sizes
    sizes = []
    while total > 6:
        sizes.append(4)
        total -= 4
    return sizes + [total]


def pack_kernel(height, parts, chunks, me_ref, in_ref, *rest):
    outs, scr = rest[:-1], rest[-1]
    comps, size_y = in_ref.shape[1], in_ref.shape[3]
    first = chunks[0][0]
    last = chunks[-1][1]
    me = me_ref[0]
    for c in range(comps):
        for start in range(0, size_y, 16):
            wanted = [
                (p, e - first, height * p - 1 + e)
                for p in range(parts)
                for e in range(first, last)
                if start <= height * p - 1 + e < start + 16
            ]
            if not wanted:
                continue
            turned = jnp.swapaxes(in_ref[:, c, 0, start : start + 16, :], 0, 1)
            for p, e, y in wanted:
                scr[p, e, c] = turned[y - start]
        for p in range(parts):
            for e in range(first, last):
                if not 0 <= height * p - 1 + e < size_y:
                    scr[p, e - first, c] = jnp.zeros(scr.shape[3:], scr.dtype)
    for r, (lo, hi) in enumerate(chunks):
        for k in range(parts):
            outs[r * parts + k][0] = scr[me ^ k, lo - first : hi - first]


def pack(modes, me, height, parts, chunks):
    local, comps, planes, size_y, size_z = modes.shape
    shapes = [
        jax.ShapeDtypeStruct((planes, hi - lo, comps, local, size_z), modes.dtype)
        for lo, hi in chunks
        for _ in range(parts)
    ]
    count = chunks[-1][1] - chunks[0][0]
    outs = pl.pallas_call(
        functools.partial(pack_kernel, height, parts, chunks),
        grid=(planes,),
        in_specs=[
            pl.BlockSpec(memory_space=pltpu.SMEM),
            pl.BlockSpec((local, comps, 1, size_y, size_z), lambda x: (0, 0, x, 0, 0)),
        ],
        out_specs=[pl.BlockSpec((1,) + s.shape[1:], lambda x: (x, 0, 0, 0, 0)) for s in shapes],
        out_shape=shapes,
        scratch_shapes=[pltpu.VMEM((parts, count, comps, local, size_z), modes.dtype)],
        compiler_params=pltpu.CompilerParams(vmem_limit_bytes=VMEM_BYTES),
        name="pack",
        cost_estimate=pl.CostEstimate(flops=0, bytes_accessed=2 * modes.size * 2, transcendentals=0),
    )(me, modes)
    return [outs[r * parts : (r + 1) * parts] for r in range(len(chunks))]


def load_kernel(first_row, prev_rows, rows, own, parts, *refs):
    if prev_rows:
        (thick_ref, tap_ref, lam_ref, s_ref, f_ref, lo_ref, hi_ref, e_ref, fp_ref, lop_ref, hip_ref, ep_ref,
         out_ref, win, other, g0, g1, l_ref, sems) = refs
    else:
        (thick_ref, tap_ref, lam_ref, f_ref, lo_ref, hi_ref, e_ref,
         out_ref, win, other, g0, g1, l_ref, sems) = refs
    planes = f_ref.shape[0]
    size_z = f_ref.shape[-1]
    width = f_ref.shape[2]
    comps = width // own
    local = own // parts
    keep = 2 if prev_rows else 0
    done = rows - 2 + keep
    started = []
    for r in range(done + 2):
        if r < keep:
            at = prev_rows - 2 + r
            sources = (fp_ref, lop_ref, hip_ref)
        else:
            at = r - keep
            sources = (f_ref, lo_ref, hi_ref)
        started += [
            pltpu.make_async_copy(sources[0].at[:, at], win.at[1 : 1 + planes, r], sems.at[r, 0]),
            pltpu.make_async_copy(sources[1].at[at], win.at[0, r], sems.at[r, 1]),
            pltpu.make_async_copy(sources[2].at[at], win.at[planes + 1, r], sems.at[r, 2]),
        ]
        if 1 <= r <= done:
            theirs = ep_ref if r < keep else e_ref
            started += [pltpu.make_async_copy(theirs.at[:, at], other.at[:, r - 1], sems.at[r, 3])]
    for copy in started:
        copy.start()

    def arrived(r):
        pltpu.make_async_copy(f_ref.at[:, 0], win.at[1 : 1 + planes, r], sems.at[r, 0]).wait()
        pltpu.make_async_copy(lo_ref.at[0], win.at[0, r], sems.at[r, 1]).wait()
        pltpu.make_async_copy(hi_ref.at[0], win.at[planes + 1, r], sems.at[r, 2]).wait()

    if prev_rows:
        out_ref[...] = s_ref[...]
    else:
        out_ref[...] = jnp.zeros_like(out_ref)

    gap = lax.broadcasted_iota(jnp.int32, (size_z, size_z), 0) - lax.broadcasted_iota(
        jnp.int32, (size_z, size_z), 1
    )
    diag = [gap == d - 1 for d in range(3)]

    def bands(g_ref, y, x, ab):
        a, b = AB[ab]
        row = first_row + y
        g = 0.5 * (thick_ref[x + 1, row + 1, 1:2] + thick_ref[x + a, row + b])
        for kind in range(2):
            coeff = tap_ref[kind, ab] * g
            high = coeff.astype(jnp.bfloat16).astype(jnp.float32)
            for half, part in enumerate((high, coeff - high)):
                band = jnp.zeros((size_z, size_z), jnp.float32)
                for d in range(3):
                    band = jnp.where(diag[d], part[d : d + 1], band)
                g_ref[
                    (2 * ab + half) * size_z : (2 * ab + half + 1) * size_z,
                    kind * size_z : (kind + 1) * size_z,
                ] = band.astype(jnp.bfloat16)

    def modes_of(block, c):
        return jnp.concatenate(
            [block[(k * comps + c) * local : (k * comps + c + 1) * local] for k in range(parts)], axis=0
        )

    for ab in range(9):
        bands(g0, 0, 0, ab)
    arrived(0)
    arrived(1)

    def row(y, _):
        arrived(y + 2)
        for x in range(planes):
            now, then = (g0, g1) if x % 2 == 0 else (g1, g0)
            images = None
            for ab, (a, b) in enumerate(AB):
                near = win[x + a, y + b]
                image = jnp.dot(
                    jnp.concatenate([near, near], axis=1),
                    now[2 * ab * size_z : 2 * (ab + 1) * size_z],
                    preferred_element_type=jnp.float32,
                )
                images = image if images is None else images + image
                if x + 1 < planes:
                    bands(then, y, x + 1, ab)
                else:
                    bands(then, jnp.minimum(y + 1, done - 1), 0, ab)
            for c in range(comps):
                image = modes_of(images, c)
                l_ref[:, (x * comps + c) * size_z : (x * comps + c + 1) * size_z] = (
                    image[:, :size_z] - lam_ref[...] * image[:, size_z:]
                ).astype(jnp.bfloat16)
        pltpu.make_async_copy(e_ref.at[:, 0], other.at[:, y], sems.at[y + 1, 3]).wait()
        cells = [(x, c) for x in range(planes) for c in range(comps)]
        mine = jnp.concatenate([modes_of(win[x + 1, y + 1], c) for x, c in cells], axis=1)
        theirs = jnp.concatenate([modes_of(other[x, y], c) for x, c in cells], axis=1)
        out_ref[...] += lax.dot_general(
            jnp.concatenate([mine, theirs], axis=0),
            l_ref[...],
            (((1,), (1,)), ((), ())),
            preferred_element_type=jnp.float32,
        )
        return 0

    lax.fori_loop(0, done, row, 0)


def load(first_row, thick, taps, lam, sums, now, before, own, parts):
    rows = now[0].shape[1]
    planes, _, width, size_z = now[0].shape
    prev_rows = before[0].shape[1] if before else 0
    done = rows if before else rows - 2
    vmem = pl.BlockSpec(memory_space=pltpu.VMEM)
    hbm = pl.BlockSpec(memory_space=pl.ANY)
    args = [thick, taps, lam] + ([sums] if before else []) + list(now) + (list(before) if before else [])
    specs = [vmem] * (4 if before else 3) + [hbm] * (8 if before else 4)
    out = jax.ShapeDtypeStruct((2 * own, own), jnp.float32)
    depth = 2 * 9 * size_z
    return pl.pallas_call(
        functools.partial(load_kernel, first_row, prev_rows, rows, own, parts),
        in_specs=specs,
        out_specs=vmem,
        out_shape=out,
        scratch_shapes=[
            pltpu.VMEM((planes + 2, done + 2, width, size_z), jnp.bfloat16),
            pltpu.VMEM((planes, done, width, size_z), jnp.bfloat16),
            pltpu.VMEM((depth, 2 * size_z), jnp.bfloat16),
            pltpu.VMEM((depth, 2 * size_z), jnp.bfloat16),
            pltpu.VMEM((own, planes * width // own * size_z), jnp.bfloat16),
            pltpu.SemaphoreType.DMA((done + 2, 4)),
        ],
        compiler_params=pltpu.CompilerParams(vmem_limit_bytes=VMEM_BYTES),
        name="load",
        cost_estimate=pl.CostEstimate(
            flops=2 * done * planes * width * depth * 2 * size_z,
            bytes_accessed=4 * done * planes * width * size_z,
            transcendentals=0,
        ),
    )(*args)


def join_kernel(parts, *refs):
    blocks, (field, lowest, highest, sems) = refs[:parts], refs[parts:]
    planes = field.shape[0]
    size = field.shape[2] // parts
    copies = []
    for k, block in enumerate(blocks):
        at = slice(k * size, (k + 1) * size)
        copies += [
            pltpu.make_async_copy(block.at[0], lowest.at[:, at], sems.at[k, 0]),
            pltpu.make_async_copy(block.at[planes - 1], highest.at[:, at], sems.at[k, 1]),
            pltpu.make_async_copy(block, field.at[:, :, at], sems.at[k, 2]),
        ]
    for copy in copies:
        copy.start()
    for copy in copies:
        copy.wait()


def join(blocks):
    planes, rows, size, size_z = blocks[0].shape
    parts = len(blocks)
    hbm = pl.BlockSpec(memory_space=pl.ANY)
    plane = jax.ShapeDtypeStruct((rows, size * parts, size_z), blocks[0].dtype)
    return pl.pallas_call(
        functools.partial(join_kernel, parts),
        in_specs=[hbm] * parts,
        out_specs=[hbm] * 3,
        out_shape=[jax.ShapeDtypeStruct((planes,) + plane.shape, plane.dtype), plane, plane],
        scratch_shapes=[pltpu.SemaphoreType.DMA((parts, 3))],
        name="join",
    )(*blocks)


def arrange_kernel(parts, local, pos_ref, s_ref, *outs):
    *outs, rows_ref = outs
    me, mine = pos_ref[0], pos_ref[1]
    own = parts * local
    for h in range(2):
        for k in range(parts):
            slot = (me ^ k) * 2 + (mine ^ h)
            rows_ref[slot] = s_ref[h * own + k * local : h * own + (k + 1) * local]
    whole = rows_ref[...].reshape(2 * own, own)
    for k, out in enumerate(outs):
        rows, lanes = out.shape
        strips = lanes // local
        out[...] = jnp.concatenate(
            [whole[n * rows : (n + 1) * rows, k * local : (k + 1) * local] for n in range(strips)], axis=1
        )


def arrange(pos, sums, parts, local, sectors):
    total, own = sums.shape
    rows = total // sectors
    return pl.pallas_call(
        functools.partial(arrange_kernel, parts, local),
        in_specs=[pl.BlockSpec(memory_space=pltpu.SMEM), pl.BlockSpec(memory_space=pltpu.VMEM)],
        out_specs=[pl.BlockSpec(memory_space=pltpu.VMEM)] * parts,
        out_shape=[jax.ShapeDtypeStruct((rows, sectors * local), jnp.float32)] * parts,
        scratch_shapes=[pltpu.VMEM((2 * parts, local, own), jnp.float32)],
        name="arrange",
    )(pos, sums)


def on_device(modes, thickness, stiff_taps, mass_taps, eigenvalues):
    local, comps, planes, size_y, size_z = modes.shape
    sectors, groups = lax.axis_size("sector"), lax.axis_size("mode")
    parts = groups // 2
    height = size_y // parts
    own = parts * local
    index = lax.axis_index("mode")
    me, mine = index // 2, index % 2

    def other_part(value, k):
        return lax.ppermute(value, "mode", [(i, i ^ (2 * k)) for i in range(groups)])

    def other_half(value):
        return lax.ppermute(value, "mode", [(i, i ^ 1) for i in range(groups)])

    def from_below(value):
        return lax.ppermute(value, "sector", [(i, i + 1) for i in range(sectors - 1)])

    def from_above(value):
        return lax.ppermute(value, "sector", [(i + 1, i) for i in range(sectors - 1)])

    bounds, at = [], 0
    for size in chunk_rows(height + 2):
        bounds.append((at, at + size))
        at += size
    me_word = me.astype(jnp.int32).reshape(1)
    packed = pack(modes, me_word, height, parts, bounds[:1])
    packed += pack(modes, me_word, height, parts, bounds[1:])

    thick = jnp.concatenate([from_below(thickness[-1:]), thickness, from_above(thickness[:1])], axis=0)
    thick = jnp.pad(thick, ((0, 0), (1, 1), (1, 1)))
    thick = lax.dynamic_slice_in_dim(thick, me * height, height + 2, axis=1)
    thick = jnp.stack([thick[:, :, d : d + size_z] for d in range(3)], axis=2)
    taps = jnp.stack([stiff_taps, mass_taps]).reshape(2, 9, 3, 1)
    taps = jnp.broadcast_to(taps, (2, 9, 3, size_z))

    lams = jnp.concatenate(
        [eigenvalues] + [other_part(eigenvalues, k) for k in range(1, parts)], axis=0
    )
    lams = jnp.broadcast_to(lams[:, None], (own, size_z))

    sums, before, at = None, None, 0
    count = len(bounds)
    received, joined = {}, {}

    def receive(r):
        received[r] = [packed[r][0]] + [other_part(packed[r][k], k) for k in range(1, parts)]

    def gather(r):
        planes_, rows_ = received[r][0].shape[:2]
        blocks = [v.reshape(planes_, rows_, comps * local, size_z) for v in received[r]]
        field, lowest, highest = join(blocks)
        joined[r] = (field, from_below(highest), from_above(lowest), other_half(field))

    for r in range(min(2, count)):
        receive(r)
    gather(0)
    sums = None
    for r in range(count):
        if r + 2 < count:
            fenced, packed[r + 2] = lax.optimization_barrier((joined[r][0], packed[r + 2]))
            joined[r] = (fenced,) + joined[r][1:]
            receive(r + 2)
        if r + 1 < count:
            if r > 0:
                received[r + 1], sums = lax.optimization_barrier((received[r + 1], sums))
            gather(r + 1)
            fenced, nearby = lax.optimization_barrier((joined[r + 1][0], joined[r][1]))
            joined[r + 1] = (fenced,) + joined[r + 1][1:]
            joined[r] = (joined[r][0], nearby) + joined[r][2:]
        before = joined[r - 1] if r else None
        done = bounds[r][1] - bounds[r][0] - (0 if r else 2)
        sums = load(at, thick, taps, lams, sums, joined[r], before, own, parts)
        at += done

    pos = jnp.stack([me, mine]).astype(jnp.int32)
    strips = arrange(pos, sums, parts, local, sectors)
    total = strips[0]
    for k in range(1, parts):
        total = total + other_part(strips[k], k)
    summed = total
    for step in range(1, sectors):
        summed = summed + lax.ppermute(
            total, "sector", [(i, (i + step) % sectors) for i in range(sectors)]
        )
    return lax.dynamic_slice_in_dim(summed, lax.axis_index("sector") * local, local, axis=1)


def solution(mesh):
    in_specs = (P("mode", None, "sector", None, None), P("sector", None, None), P(), P(), P("mode"))
    out_specs = P("sector", "mode")
    return jax.shard_map(
        on_device, mesh=mesh, in_specs=in_specs, out_specs=out_specs, check_vma=False
    )
```

```python
import functools

import jax
import jax.numpy as jnp
from jax import lax
from jax.experimental import pallas as pl
from jax.experimental.pallas import tpu as pltpu
from jax.sharding import PartitionSpec as P

VMEM_BYTES = 56 * 1024 * 1024
AB = [(a, b) for a in range(3) for b in range(3)]


def chunk_rows(total):
    sizes = [4, 6, 6, 6]
    if sum(sizes) == total:
        return sizes
    sizes = []
    while total > 6:
        sizes.append(4)
        total -= 4
    return sizes + [total]


def pack_kernel(height, parts, chunks, me_ref, in_ref, *rest):
    outs, scr = rest[:-1], rest[-1]
    comps, size_y = in_ref.shape[1], in_ref.shape[3]
    first = chunks[0][0]
    last = chunks[-1][1]
    me = me_ref[0]
    for c in range(comps):
        for start in range(0, size_y, 16):
            wanted = [
                (p, e - first, height * p - 1 + e)
                for p in range(parts)
                for e in range(first, last)
                if start <= height * p - 1 + e < start + 16
            ]
            if not wanted:
                continue
            turned = jnp.swapaxes(in_ref[:, c, 0, start : start + 16, :], 0, 1)
            for p, e, y in wanted:
                scr[p, e, c] = turned[y - start]
        for p in range(parts):
            for e in range(first, last):
                if not 0 <= height * p - 1 + e < size_y:
                    scr[p, e - first, c] = jnp.zeros(scr.shape[3:], scr.dtype)
    for r, (lo, hi) in enumerate(chunks):
        for k in range(parts):
            outs[r * parts + k][0] = scr[me ^ k, lo - first : hi - first]


def pack(modes, me, height, parts, chunks):
    local, comps, planes, size_y, size_z = modes.shape
    shapes = [
        jax.ShapeDtypeStruct((planes, hi - lo, comps, local, size_z), modes.dtype)
        for lo, hi in chunks
        for _ in range(parts)
    ]
    count = chunks[-1][1] - chunks[0][0]
    outs = pl.pallas_call(
        functools.partial(pack_kernel, height, parts, chunks),
        grid=(planes,),
        in_specs=[
            pl.BlockSpec(memory_space=pltpu.SMEM),
            pl.BlockSpec((local, comps, 1, size_y, size_z), lambda x: (0, 0, x, 0, 0)),
        ],
        out_specs=[pl.BlockSpec((1,) + s.shape[1:], lambda x: (x, 0, 0, 0, 0)) for s in shapes],
        out_shape=shapes,
        scratch_shapes=[pltpu.VMEM((parts, count, comps, local, size_z), modes.dtype)],
        compiler_params=pltpu.CompilerParams(vmem_limit_bytes=VMEM_BYTES),
        name="pack",
        cost_estimate=pl.CostEstimate(flops=0, bytes_accessed=2 * modes.size * 2, transcendentals=0),
    )(me, modes)
    return [outs[r * parts : (r + 1) * parts] for r in range(len(chunks))]


def load_kernel(first_row, prev_rows, rows, own, parts, *refs):
    if prev_rows:
        (thick_ref, tap_ref, lam_ref, s_ref, f_ref, lo_ref, hi_ref, e_ref, fp_ref, lop_ref, hip_ref, ep_ref,
         out_ref, win, other, g0, g1, l_ref, sems) = refs
    else:
        (thick_ref, tap_ref, lam_ref, f_ref, lo_ref, hi_ref, e_ref,
         out_ref, win, other, g0, g1, l_ref, sems) = refs
    planes = f_ref.shape[0]
    size_z = f_ref.shape[-1]
    width = f_ref.shape[2]
    comps = width // own
    local = own // parts
    keep = 2 if prev_rows else 0
    done = rows - 2 + keep
    started = []
    for r in range(done + 2):
        if r < keep:
            at = prev_rows - 2 + r
            sources = (fp_ref, lop_ref, hip_ref)
        else:
            at = r - keep
            sources = (f_ref, lo_ref, hi_ref)
        started += [
            pltpu.make_async_copy(sources[0].at[:, at], win.at[1 : 1 + planes, r], sems.at[r, 0]),
            pltpu.make_async_copy(sources[1].at[at], win.at[0, r], sems.at[r, 1]),
            pltpu.make_async_copy(sources[2].at[at], win.at[planes + 1, r], sems.at[r, 2]),
        ]
        if 1 <= r <= done:
            theirs = ep_ref if r < keep else e_ref
            started += [pltpu.make_async_copy(theirs.at[:, at], other.at[:, r - 1], sems.at[r, 3])]
    for copy in started:
        copy.start()

    def arrived(r):
        pltpu.make_async_copy(f_ref.at[:, 0], win.at[1 : 1 + planes, r], sems.at[r, 0]).wait()
        pltpu.make_async_copy(lo_ref.at[0], win.at[0, r], sems.at[r, 1]).wait()
        pltpu.make_async_copy(hi_ref.at[0], win.at[planes + 1, r], sems.at[r, 2]).wait()

    if prev_rows:
        out_ref[...] = s_ref[...]
    else:
        out_ref[...] = jnp.zeros_like(out_ref)

    rows_16 = lax.broadcasted_iota(jnp.int32, (16, size_z), 0)
    lanes_16 = lax.broadcasted_iota(jnp.int32, (16, size_z), 1)
    turn = lax.rem(rows_16 - lanes_16 + 16 * size_z + 1, 16)
    diag = [turn == d for d in range(3)]
    gap = lax.broadcasted_iota(jnp.int32, (size_z, size_z), 0) - lax.broadcasted_iota(
        jnp.int32, (size_z, size_z), 1
    )
    near_diag = jnp.where(jnp.abs(gap) <= 1, 1.0, 0.0).astype(jnp.bfloat16)

    def bands(g_ref, y, x, ab):
        a, b = AB[ab]
        row = first_row + y
        g = 0.5 * (thick_ref[x + 1, row + 1, 1:2] + thick_ref[x + a, row + b])
        for kind in range(2):
            coeff = tap_ref[kind, ab] * g
            high = coeff.astype(jnp.bfloat16).astype(jnp.float32)
            for half, part in enumerate((high, coeff - high)):
                strip = jnp.zeros((16, size_z), jnp.float32)
                for d in range(3):
                    strip = jnp.where(diag[d], part[d : d + 1], strip)
                strip = strip.astype(jnp.bfloat16)
                g_ref[
                    (2 * ab + half) * size_z : (2 * ab + half + 1) * size_z,
                    kind * size_z : (kind + 1) * size_z,
                ] = jnp.concatenate([strip] * (size_z // 16), axis=0) * near_diag

    def modes_of(block, c):
        return jnp.concatenate(
            [block[(k * comps + c) * local : (k * comps + c + 1) * local] for k in range(parts)], axis=0
        )

    for ab in range(9):
        bands(g0, 0, 0, ab)
    arrived(0)
    arrived(1)

    def row(y, _):
        arrived(y + 2)
        for x in range(planes):
            now, then = (g0, g1) if x % 2 == 0 else (g1, g0)
            images = None
            for ab, (a, b) in enumerate(AB):
                near = win[x + a, y + b]
                image = jnp.dot(
                    jnp.concatenate([near, near], axis=1),
                    now[2 * ab * size_z : 2 * (ab + 1) * size_z],
                    preferred_element_type=jnp.float32,
                )
                images = image if images is None else images + image
                if x + 1 < planes:
                    bands(then, y, x + 1, ab)
                else:
                    bands(then, jnp.minimum(y + 1, done - 1), 0, ab)
            for c in range(comps):
                image = modes_of(images, c)
                l_ref[:, (x * comps + c) * size_z : (x * comps + c + 1) * size_z] = (
                    image[:, :size_z] - lam_ref[...] * image[:, size_z:]
                ).astype(jnp.bfloat16)
        pltpu.make_async_copy(e_ref.at[:, 0], other.at[:, y], sems.at[y + 1, 3]).wait()
        cells = [(x, c) for x in range(planes) for c in range(comps)]
        mine = jnp.concatenate([modes_of(win[x + 1, y + 1], c) for x, c in cells], axis=1)
        theirs = jnp.concatenate([modes_of(other[x, y], c) for x, c in cells], axis=1)
        out_ref[...] += lax.dot_general(
            jnp.concatenate([mine, theirs], axis=0),
            l_ref[...],
            (((1,), (1,)), ((), ())),
            preferred_element_type=jnp.float32,
        )
        return 0

    lax.fori_loop(0, done, row, 0)


def load(first_row, thick, taps, lam, sums, now, before, own, parts):
    rows = now[0].shape[1]
    planes, _, width, size_z = now[0].shape
    prev_rows = before[0].shape[1] if before else 0
    done = rows if before else rows - 2
    vmem = pl.BlockSpec(memory_space=pltpu.VMEM)
    hbm = pl.BlockSpec(memory_space=pl.ANY)
    args = [thick, taps, lam] + ([sums] if before else []) + list(now) + (list(before) if before else [])
    specs = [vmem] * (4 if before else 3) + [hbm] * (8 if before else 4)
    out = jax.ShapeDtypeStruct((2 * own, own), jnp.float32)
    depth = 2 * 9 * size_z
    return pl.pallas_call(
        functools.partial(load_kernel, first_row, prev_rows, rows, own, parts),
        in_specs=specs,
        out_specs=vmem,
        out_shape=out,
        scratch_shapes=[
            pltpu.VMEM((planes + 2, done + 2, width, size_z), jnp.bfloat16),
            pltpu.VMEM((planes, done, width, size_z), jnp.bfloat16),
            pltpu.VMEM((depth, 2 * size_z), jnp.bfloat16),
            pltpu.VMEM((depth, 2 * size_z), jnp.bfloat16),
            pltpu.VMEM((own, planes * width // own * size_z), jnp.bfloat16),
            pltpu.SemaphoreType.DMA((done + 2, 4)),
        ],
        compiler_params=pltpu.CompilerParams(vmem_limit_bytes=VMEM_BYTES),
        name="load",
        cost_estimate=pl.CostEstimate(
            flops=50000000000,
            bytes_accessed=4 * done * planes * width * size_z,
            transcendentals=0,
        ),
    )(*args)


def join_kernel(parts, *refs):
    blocks, (field, lowest, highest, held, in_sems, out_sems) = refs[:parts], refs[parts:]
    planes = field.shape[0]
    size = field.shape[2] // parts
    order = [0, planes - 1] + list(range(1, planes - 1))
    arrivals = {
        x: [
            pltpu.make_async_copy(block.at[x], held.at[x, :, k * size : (k + 1) * size], in_sems.at[x, k])
            for k, block in enumerate(blocks)
        ]
        for x in order
    }
    for x in order:
        for copy in arrivals[x]:
            copy.start()
    leaving = []
    for x in order:
        for copy in arrivals[x]:
            copy.wait()
        if x == 0:
            leaving.append(pltpu.make_async_copy(held.at[x], lowest, out_sems.at[planes]))
            leaving[-1].start()
        if x == planes - 1:
            leaving.append(pltpu.make_async_copy(held.at[x], highest, out_sems.at[planes + 1]))
            leaving[-1].start()
        leaving.append(pltpu.make_async_copy(held.at[x], field.at[x], out_sems.at[x]))
        leaving[-1].start()
    for copy in leaving:
        copy.wait()


def join(blocks):
    planes, rows, size, size_z = blocks[0].shape
    parts = len(blocks)
    hbm = pl.BlockSpec(memory_space=pl.ANY)
    plane = jax.ShapeDtypeStruct((rows, size * parts, size_z), blocks[0].dtype)
    field = jax.ShapeDtypeStruct((planes,) + plane.shape, plane.dtype)
    return pl.pallas_call(
        functools.partial(join_kernel, parts),
        in_specs=[hbm] * parts,
        out_specs=[hbm] * 3,
        out_shape=[field, plane, plane],
        scratch_shapes=[
            pltpu.VMEM(field.shape, field.dtype),
            pltpu.SemaphoreType.DMA((planes, parts)),
            pltpu.SemaphoreType.DMA((planes + 2,)),
        ],
        compiler_params=pltpu.CompilerParams(vmem_limit_bytes=VMEM_BYTES),
        name="join",
        cost_estimate=pl.CostEstimate(
            flops=50000000000, bytes_accessed=0, transcendentals=0
        ),
    )(*blocks)


def arrange_kernel(parts, local, pos_ref, s_ref, *outs):
    *outs, rows_ref = outs
    me, mine = pos_ref[0], pos_ref[1]
    own = parts * local
    for h in range(2):
        for k in range(parts):
            slot = (me ^ k) * 2 + (mine ^ h)
            rows_ref[slot] = s_ref[h * own + k * local : h * own + (k + 1) * local]
    whole = rows_ref[...].reshape(2 * own, own)
    for k, out in enumerate(outs):
        rows, lanes = out.shape
        strips = lanes // local
        out[...] = jnp.concatenate(
            [whole[n * rows : (n + 1) * rows, k * local : (k + 1) * local] for n in range(strips)], axis=1
        )


def arrange(pos, sums, parts, local, sectors):
    total, own = sums.shape
    rows = total // sectors
    return pl.pallas_call(
        functools.partial(arrange_kernel, parts, local),
        in_specs=[pl.BlockSpec(memory_space=pltpu.SMEM), pl.BlockSpec(memory_space=pltpu.VMEM)],
        out_specs=[pl.BlockSpec(memory_space=pltpu.VMEM)] * parts,
        out_shape=[jax.ShapeDtypeStruct((rows, sectors * local), jnp.float32)] * parts,
        scratch_shapes=[pltpu.VMEM((2 * parts, local, own), jnp.float32)],
        name="arrange",
    )(pos, sums)


def on_device(modes, thickness, stiff_taps, mass_taps, eigenvalues):
    local, comps, planes, size_y, size_z = modes.shape
    sectors, groups = lax.axis_size("sector"), lax.axis_size("mode")
    parts = groups // 2
    height = size_y // parts
    own = parts * local
    index = lax.axis_index("mode")
    me, mine = index // 2, index % 2

    def other_part(value, k, name="pre"):
        with jax.named_scope(f"{name}_{k}"):
            return lax.ppermute(value, "mode", [(i, i ^ (2 * k)) for i in range(groups)])

    def other_half(value, name="core"):
        with jax.named_scope(name):
            return lax.ppermute(value, "mode", [(i, i ^ 1) for i in range(groups)])

    def from_below(value, name="pre_lo"):
        with jax.named_scope(name):
            return lax.ppermute(value, "sector", [(i, i + 1) for i in range(sectors - 1)])

    def from_above(value, name="pre_hi"):
        with jax.named_scope(name):
            return lax.ppermute(value, "sector", [(i + 1, i) for i in range(sectors - 1)])

    bounds, at = [], 0
    for size in chunk_rows(height + 2):
        bounds.append((at, at + size))
        at += size
    me_word = me.astype(jnp.int32).reshape(1)
    packed = pack(modes, me_word, height, parts, bounds[:1])
    packed += pack(modes, me_word, height, parts, bounds[1:])

    thick = jnp.concatenate([from_below(thickness[-1:]), thickness, from_above(thickness[:1])], axis=0)
    thick = jnp.pad(thick, ((0, 0), (1, 1), (1, 1)))
    thick = lax.dynamic_slice_in_dim(thick, me * height, height + 2, axis=1)
    thick = jnp.stack([thick[:, :, d : d + size_z] for d in range(3)], axis=2)
    taps = jnp.stack([stiff_taps, mass_taps]).reshape(2, 9, 3, 1)
    taps = jnp.broadcast_to(taps, (2, 9, 3, size_z))

    with jax.named_scope("pre_eig"):
        held_back, packed[0] = lax.optimization_barrier((eigenvalues, packed[0]))
        lams = lax.all_to_all(
            jnp.broadcast_to(held_back[None], (groups, local)), "mode", 0, 0, tiled=True
        )
    lams = lams.reshape(parts, 2, local)
    lams = lax.dynamic_index_in_dim(lams, mine, 1, keepdims=False)
    lams = jnp.concatenate(
        [lax.dynamic_index_in_dim(lams, me ^ k, 0, keepdims=False) for k in range(parts)], axis=0
    )
    lams = jnp.broadcast_to(lams[:, None], (own, size_z))

    count = len(bounds)
    received, joined = {}, {}

    def receive(r):
        received[r] = [packed[r][0]] + [other_part(packed[r][k], k, f"xy{r}") for k in range(1, parts)]

    def gather(r):
        planes_, rows_ = received[r][0].shape[:2]
        blocks = [v.reshape(planes_, rows_, comps * local, size_z) for v in received[r]]
        field, lowest, highest = join(blocks)
        joined[r] = (
            field,
            from_below(highest, f"z{r}_lo"),
            from_above(lowest, f"z{r}_hi"),
            other_half(field, f"core{r}"),
        )

    for r in range(min(2, count)):
        receive(r)
    received[0], thick, taps, packed[1:] = lax.optimization_barrier(
        (received[0], thick, taps, packed[1:])
    )
    sums, at = None, 0

    def follow(r):
        if r + 2 < count:
            received[r], packed[r + 2] = lax.optimization_barrier((received[r], packed[r + 2]))
            receive(r + 2)

    follow(0)
    gather(0)
    for r in range(count):
        if r + 1 < count:
            field, lowest, highest, theirs = joined[r]
            received[r + 1], lowest, highest, sums = lax.optimization_barrier(
                (received[r + 1], lowest, highest, sums)
            )
            follow(r + 1)
            gather(r + 1)
            fenced, lowest = lax.optimization_barrier((joined[r + 1][0], lowest))
            joined[r + 1] = (fenced,) + joined[r + 1][1:]
            joined[r] = (field, lowest, highest, theirs)
        before = joined[r - 1] if r else None
        done = bounds[r][1] - bounds[r][0] - (0 if r else 2)
        sums = load(at, thick, taps, lams, sums, joined[r], before, own, parts)
        at += done

    pos = jnp.stack([me, mine]).astype(jnp.int32)
    strips = arrange(pos, sums, parts, local, sectors)
    total = strips[0]
    for k in range(1, parts):
        total = total + other_part(strips[k], k, "fin")
    summed = total
    for step in range(1, sectors):
        summed = summed + lax.ppermute(
            total, "sector", [(i, (i + step) % sectors) for i in range(sectors)]
        )
    return lax.dynamic_slice_in_dim(summed, lax.axis_index("sector") * local, local, axis=1)


def solution(mesh):
    in_specs = (P("mode", None, "sector", None, None), P("sector", None, None), P(), P(), P("mode"))
    out_specs = P("sector", "mode")
    return jax.shard_map(
        on_device, mesh=mesh, in_specs=in_specs, out_specs=out_specs, check_vma=False
    )
```

```python
import functools

import jax
import jax.numpy as jnp
from jax import lax
from jax.experimental import pallas as pl
from jax.experimental.pallas import tpu as pltpu
from jax.sharding import PartitionSpec as P

VMEM_BYTES = 56 * 1024 * 1024
AB = [(a, b) for a in range(3) for b in range(3)]


def chunk_rows(total):
    sizes = [4, 6, 6, 6]
    if sum(sizes) == total:
        return sizes
    sizes = []
    while total > 6:
        sizes.append(4)
        total -= 4
    return sizes + [total]


def pack_kernel(height, parts, chunks, me_ref, in_ref, *rest):
    outs, scr = rest[:-1], rest[-1]
    comps, size_y = in_ref.shape[1], in_ref.shape[3]
    first = chunks[0][0]
    last = chunks[-1][1]
    me = me_ref[0]
    for c in range(comps):
        for start in range(0, size_y, 16):
            wanted = [
                (p, e - first, height * p - 1 + e)
                for p in range(parts)
                for e in range(first, last)
                if start <= height * p - 1 + e < start + 16
            ]
            if not wanted:
                continue
            turned = jnp.swapaxes(in_ref[:, c, 0, start : start + 16, :], 0, 1)
            for p, e, y in wanted:
                scr[p, e, c] = turned[y - start]
        for p in range(parts):
            for e in range(first, last):
                if not 0 <= height * p - 1 + e < size_y:
                    scr[p, e - first, c] = jnp.zeros(scr.shape[3:], scr.dtype)
    for r, (lo, hi) in enumerate(chunks):
        for k in range(parts):
            outs[r * parts + k][0] = scr[me ^ k, lo - first : hi - first]


def pack(modes, me, height, parts, chunks):
    local, comps, planes, size_y, size_z = modes.shape
    shapes = [
        jax.ShapeDtypeStruct((planes, hi - lo, comps, local, size_z), modes.dtype)
        for lo, hi in chunks
        for _ in range(parts)
    ]
    count = chunks[-1][1] - chunks[0][0]
    outs = pl.pallas_call(
        functools.partial(pack_kernel, height, parts, chunks),
        grid=(planes,),
        in_specs=[
            pl.BlockSpec(memory_space=pltpu.SMEM),
            pl.BlockSpec((local, comps, 1, size_y, size_z), lambda x: (0, 0, x, 0, 0)),
        ],
        out_specs=[pl.BlockSpec((1,) + s.shape[1:], lambda x: (x, 0, 0, 0, 0)) for s in shapes],
        out_shape=shapes,
        scratch_shapes=[pltpu.VMEM((parts, count, comps, local, size_z), modes.dtype)],
        compiler_params=pltpu.CompilerParams(vmem_limit_bytes=VMEM_BYTES),
        name="pack",
        cost_estimate=pl.CostEstimate(flops=0, bytes_accessed=2 * modes.size * 2, transcendentals=0),
    )(me, modes)
    return [outs[r * parts : (r + 1) * parts] for r in range(len(chunks))]


def load_kernel(first_row, prev_rows, rows, own, parts, *refs):
    if prev_rows:
        (thick_ref, tap_ref, lam_ref, s_ref, f_ref, lo_ref, hi_ref, e_ref, fp_ref, lop_ref, hip_ref, ep_ref,
         out_ref, win, other, g0, g1, l0, l1, sems) = refs
    else:
        (thick_ref, tap_ref, lam_ref, f_ref, lo_ref, hi_ref, e_ref,
         out_ref, win, other, g0, g1, l0, l1, sems) = refs
    planes = f_ref.shape[0]
    size_z = f_ref.shape[-1]
    width = f_ref.shape[2]
    comps = width // own
    local = own // parts
    keep = 2 if prev_rows else 0
    done = rows - 2 + keep
    started = []
    for r in range(done + 2):
        if r < keep:
            at = prev_rows - 2 + r
            sources = (fp_ref, lop_ref, hip_ref)
        else:
            at = r - keep
            sources = (f_ref, lo_ref, hi_ref)
        started += [
            pltpu.make_async_copy(sources[0].at[:, at], win.at[1 : 1 + planes, r], sems.at[r, 0]),
            pltpu.make_async_copy(sources[1].at[at], win.at[0, r], sems.at[r, 1]),
            pltpu.make_async_copy(sources[2].at[at], win.at[planes + 1, r], sems.at[r, 2]),
        ]
        if 1 <= r <= done:
            theirs = ep_ref if r < keep else e_ref
            started += [pltpu.make_async_copy(theirs.at[:, at], other.at[:, r - 1], sems.at[r, 3])]
    for copy in started:
        copy.start()

    def arrived(r):
        pltpu.make_async_copy(f_ref.at[:, 0], win.at[1 : 1 + planes, r], sems.at[r, 0]).wait()
        pltpu.make_async_copy(lo_ref.at[0], win.at[0, r], sems.at[r, 1]).wait()
        pltpu.make_async_copy(hi_ref.at[0], win.at[planes + 1, r], sems.at[r, 2]).wait()

    if prev_rows:
        out_ref[...] = s_ref[...]
    else:
        out_ref[...] = jnp.zeros_like(out_ref)

    rows_16 = lax.broadcasted_iota(jnp.int32, (16, size_z), 0)
    lanes_16 = lax.broadcasted_iota(jnp.int32, (16, size_z), 1)
    turn = lax.rem(rows_16 - lanes_16 + 16 * size_z + 1, 16)
    diag = [turn == d for d in range(3)]
    gap = lax.broadcasted_iota(jnp.int32, (size_z, size_z), 0) - lax.broadcasted_iota(
        jnp.int32, (size_z, size_z), 1
    )
    near_diag = jnp.where(jnp.abs(gap) <= 1, 1.0, 0.0).astype(jnp.bfloat16)

    def bands(g_ref, y, x, ab):
        a, b = AB[ab]
        row = first_row + y
        g = 0.5 * (thick_ref[x + 1, row + 1, 1:2] + thick_ref[x + a, row + b])
        for kind in range(2):
            coeff = tap_ref[kind, ab] * g
            high = coeff.astype(jnp.bfloat16).astype(jnp.float32)
            for half, part in enumerate((high, coeff - high)):
                strip = jnp.zeros((16, size_z), jnp.float32)
                for d in range(3):
                    strip = jnp.where(diag[d], part[d : d + 1], strip)
                strip = strip.astype(jnp.bfloat16)
                g_ref[
                    (2 * ab + half) * size_z : (2 * ab + half + 1) * size_z,
                    kind * size_z : (kind + 1) * size_z,
                ] = jnp.concatenate([strip] * (size_z // 16), axis=0) * near_diag

    def modes_of(block, c):
        return jnp.concatenate(
            [block[(k * comps + c) * local : (k * comps + c + 1) * local] for k in range(parts)], axis=0
        )

    cells = [(x, c) for x in range(planes) for c in range(comps)]

    def gather_sums(y, l_ref):
        mine = jnp.concatenate([modes_of(win[x + 1, y + 1], c) for x, c in cells], axis=1)
        theirs = jnp.concatenate([modes_of(other[x, y], c) for x, c in cells], axis=1)
        out_ref[...] += lax.dot_general(
            jnp.concatenate([mine, theirs], axis=0),
            l_ref[...],
            (((1,), (1,)), ((), ())),
            preferred_element_type=jnp.float32,
        )

    def stencils(y, l_ref):
        for x in range(planes):
            now, then = (g0, g1) if x % 2 == 0 else (g1, g0)
            images = None
            for ab, (a, b) in enumerate(AB):
                near = win[x + a, y + b]
                image = jnp.dot(
                    jnp.concatenate([near, near], axis=1),
                    now[2 * ab * size_z : 2 * (ab + 1) * size_z],
                    preferred_element_type=jnp.float32,
                )
                images = image if images is None else images + image
                if x + 1 < planes:
                    bands(then, y, x + 1, ab)
                else:
                    bands(then, jnp.minimum(y + 1, done - 1), 0, ab)
            for c in range(comps):
                image = modes_of(images, c)
                l_ref[:, (x * comps + c) * size_z : (x * comps + c + 1) * size_z] = (
                    image[:, :size_z] - lam_ref[...] * image[:, size_z:]
                ).astype(jnp.bfloat16)

    def other_arrived(y):
        pltpu.make_async_copy(e_ref.at[:, 0], other.at[:, y], sems.at[y + 1, 3]).wait()

    for ab in range(9):
        bands(g0, 0, 0, ab)
    arrived(0)
    arrived(1)
    other_arrived(0)
    l1[...] = jnp.zeros_like(l1)

    def two_rows(n, _):
        y = 2 * n
        arrived(y + 2)
        arrived(y + 3)
        gather_sums(jnp.maximum(y - 1, 0), l1)
        stencils(y, l0)
        gather_sums(y, l0)
        stencils(y + 1, l1)
        other_arrived(y + 1)

        @pl.when(y + 2 < done)
        def _():
            other_arrived(y + 2)

        return 0

    lax.fori_loop(0, done // 2, two_rows, 0)
    gather_sums(done - 1, l1)


def load(first_row, thick, taps, lam, sums, now, before, own, parts):
    rows = now[0].shape[1]
    planes, _, width, size_z = now[0].shape
    prev_rows = before[0].shape[1] if before else 0
    done = rows if before else rows - 2
    vmem = pl.BlockSpec(memory_space=pltpu.VMEM)
    hbm = pl.BlockSpec(memory_space=pl.ANY)
    args = [thick, taps, lam] + ([sums] if before else []) + list(now) + (list(before) if before else [])
    specs = [vmem] * (4 if before else 3) + [hbm] * (8 if before else 4)
    out = jax.ShapeDtypeStruct((2 * own, own), jnp.float32)
    depth = 2 * 9 * size_z
    return pl.pallas_call(
        functools.partial(load_kernel, first_row, prev_rows, rows, own, parts),
        in_specs=specs,
        out_specs=vmem,
        out_shape=out,
        scratch_shapes=[
            pltpu.VMEM((planes + 2, done + 2, width, size_z), jnp.bfloat16),
            pltpu.VMEM((planes, done, width, size_z), jnp.bfloat16),
            pltpu.VMEM((depth, 2 * size_z), jnp.bfloat16),
            pltpu.VMEM((depth, 2 * size_z), jnp.bfloat16),
            pltpu.VMEM((own, planes * width // own * size_z), jnp.bfloat16),
            pltpu.VMEM((own, planes * width // own * size_z), jnp.bfloat16),
            pltpu.SemaphoreType.DMA((done + 2, 4)),
        ],
        compiler_params=pltpu.CompilerParams(vmem_limit_bytes=VMEM_BYTES),
        name="load",
        cost_estimate=pl.CostEstimate(
            flops=50000000000,
            bytes_accessed=4 * done * planes * width * size_z,
            transcendentals=0,
        ),
    )(*args)


def join_kernel(parts, *refs):
    blocks, (field, lowest, highest, held, in_sems, out_sems) = refs[:parts], refs[parts:]
    planes = field.shape[0]
    size = field.shape[2] // parts
    order = [0, planes - 1] + list(range(1, planes - 1))
    arrivals = {
        x: [
            pltpu.make_async_copy(block.at[x], held.at[x, :, k * size : (k + 1) * size], in_sems.at[x, k])
            for k, block in enumerate(blocks)
        ]
        for x in order
    }
    for x in order:
        for copy in arrivals[x]:
            copy.start()
    leaving = []
    for x in order:
        for copy in arrivals[x]:
            copy.wait()
        if x == 0:
            leaving.append(pltpu.make_async_copy(held.at[x], lowest, out_sems.at[planes]))
            leaving[-1].start()
        if x == planes - 1:
            leaving.append(pltpu.make_async_copy(held.at[x], highest, out_sems.at[planes + 1]))
            leaving[-1].start()
        leaving.append(pltpu.make_async_copy(held.at[x], field.at[x], out_sems.at[x]))
        leaving[-1].start()
    for copy in leaving:
        copy.wait()


def join(blocks):
    planes, rows, size, size_z = blocks[0].shape
    parts = len(blocks)
    hbm = pl.BlockSpec(memory_space=pl.ANY)
    plane = jax.ShapeDtypeStruct((rows, size * parts, size_z), blocks[0].dtype)
    field = jax.ShapeDtypeStruct((planes,) + plane.shape, plane.dtype)
    return pl.pallas_call(
        functools.partial(join_kernel, parts),
        in_specs=[hbm] * parts,
        out_specs=[hbm] * 3,
        out_shape=[field, plane, plane],
        scratch_shapes=[
            pltpu.VMEM(field.shape, field.dtype),
            pltpu.SemaphoreType.DMA((planes, parts)),
            pltpu.SemaphoreType.DMA((planes + 2,)),
        ],
        compiler_params=pltpu.CompilerParams(vmem_limit_bytes=VMEM_BYTES),
        name="join",
        cost_estimate=pl.CostEstimate(
            flops=50000000000, bytes_accessed=0, transcendentals=0
        ),
    )(*blocks)


def arrange_kernel(parts, local, pos_ref, s_ref, *outs):
    *outs, rows_ref = outs
    me, mine = pos_ref[0], pos_ref[1]
    own = parts * local
    for h in range(2):
        for k in range(parts):
            slot = (me ^ k) * 2 + (mine ^ h)
            rows_ref[slot] = s_ref[h * own + k * local : h * own + (k + 1) * local]
    whole = rows_ref[...].reshape(2 * own, own)
    for k, out in enumerate(outs):
        rows, lanes = out.shape
        strips = lanes // local
        out[...] = jnp.concatenate(
            [whole[n * rows : (n + 1) * rows, k * local : (k + 1) * local] for n in range(strips)], axis=1
        )


def arrange(pos, sums, parts, local, sectors):
    total, own = sums.shape
    rows = total // sectors
    return pl.pallas_call(
        functools.partial(arrange_kernel, parts, local),
        in_specs=[pl.BlockSpec(memory_space=pltpu.SMEM), pl.BlockSpec(memory_space=pltpu.VMEM)],
        out_specs=[pl.BlockSpec(memory_space=pltpu.VMEM)] * parts,
        out_shape=[jax.ShapeDtypeStruct((rows, sectors * local), jnp.float32)] * parts,
        scratch_shapes=[pltpu.VMEM((2 * parts, local, own), jnp.float32)],
        name="arrange",
    )(pos, sums)


def on_device(modes, thickness, stiff_taps, mass_taps, eigenvalues):
    local, comps, planes, size_y, size_z = modes.shape
    sectors, groups = lax.axis_size("sector"), lax.axis_size("mode")
    parts = groups // 2
    height = size_y // parts
    own = parts * local
    index = lax.axis_index("mode")
    me, mine = index // 2, index % 2

    def other_part(value, k, name="pre"):
        with jax.named_scope(f"{name}_{k}"):
            return lax.ppermute(value, "mode", [(i, i ^ (2 * k)) for i in range(groups)])

    def other_half(value, name="core"):
        with jax.named_scope(name):
            return lax.ppermute(value, "mode", [(i, i ^ 1) for i in range(groups)])

    def from_below(value, name="pre_lo"):
        with jax.named_scope(name):
            return lax.ppermute(value, "sector", [(i, i + 1) for i in range(sectors - 1)])

    def from_above(value, name="pre_hi"):
        with jax.named_scope(name):
            return lax.ppermute(value, "sector", [(i + 1, i) for i in range(sectors - 1)])

    bounds, at = [], 0
    for size in chunk_rows(height + 2):
        bounds.append((at, at + size))
        at += size
    me_word = me.astype(jnp.int32).reshape(1)
    packed = pack(modes, me_word, height, parts, bounds[:1])
    packed += pack(modes, me_word, height, parts, bounds[1:])

    thick = jnp.concatenate([from_below(thickness[-1:]), thickness, from_above(thickness[:1])], axis=0)
    thick = jnp.pad(thick, ((0, 0), (1, 1), (1, 1)))
    thick = lax.dynamic_slice_in_dim(thick, me * height, height + 2, axis=1)
    thick = jnp.stack([thick[:, :, d : d + size_z] for d in range(3)], axis=2)
    taps = jnp.stack([stiff_taps, mass_taps]).reshape(2, 9, 3, 1)
    taps = jnp.broadcast_to(taps, (2, 9, 3, size_z))

    with jax.named_scope("pre_eig"):
        held_back, packed[0] = lax.optimization_barrier((eigenvalues, packed[0]))
        lams = lax.all_to_all(
            jnp.broadcast_to(held_back[None], (groups, local)), "mode", 0, 0, tiled=True
        )
    lams = lams.reshape(parts, 2, local)
    lams = lax.dynamic_index_in_dim(lams, mine, 1, keepdims=False)
    lams = jnp.concatenate(
        [lax.dynamic_index_in_dim(lams, me ^ k, 0, keepdims=False) for k in range(parts)], axis=0
    )
    lams = jnp.broadcast_to(lams[:, None], (own, size_z))

    count = len(bounds)
    received, joined = {}, {}

    def receive(r):
        received[r] = [packed[r][0]] + [other_part(packed[r][k], k, f"xy{r}") for k in range(1, parts)]

    def gather(r):
        planes_, rows_ = received[r][0].shape[:2]
        blocks = [v.reshape(planes_, rows_, comps * local, size_z) for v in received[r]]
        field, lowest, highest = join(blocks)
        joined[r] = (
            field,
            from_below(highest, f"z{r}_lo"),
            from_above(lowest, f"z{r}_hi"),
            other_half(field, f"core{r}"),
        )

    for r in range(min(2, count)):
        receive(r)
    received[0], thick, taps, packed[1:] = lax.optimization_barrier(
        (received[0], thick, taps, packed[1:])
    )
    sums, at = None, 0

    def follow(r):
        if r + 2 < count:
            received[r], packed[r + 2] = lax.optimization_barrier((received[r], packed[r + 2]))
            receive(r + 2)

    follow(0)
    gather(0)
    for r in range(count):
        if r + 1 < count:
            field, lowest, highest, theirs = joined[r]
            received[r + 1], lowest, highest, sums = lax.optimization_barrier(
                (received[r + 1], lowest, highest, sums)
            )
            follow(r + 1)
            gather(r + 1)
            fenced, lowest = lax.optimization_barrier((joined[r + 1][0], lowest))
            joined[r + 1] = (fenced,) + joined[r + 1][1:]
            joined[r] = (field, lowest, highest, theirs)
        before = joined[r - 1] if r else None
        done = bounds[r][1] - bounds[r][0] - (0 if r else 2)
        sums = load(at, thick, taps, lams, sums, joined[r], before, own, parts)
        at += done

    pos = jnp.stack([me, mine]).astype(jnp.int32)
    strips = arrange(pos, sums, parts, local, sectors)
    total = strips[0]
    for k in range(1, parts):
        total = total + other_part(strips[k], k, "fin")
    summed = total
    for step in range(1, sectors):
        summed = summed + lax.ppermute(
            total, "sector", [(i, (i + step) % sectors) for i in range(sectors)]
        )
    return lax.dynamic_slice_in_dim(summed, lax.axis_index("sector") * local, local, axis=1)


def solution(mesh):
    in_specs = (P("mode", None, "sector", None, None), P("sector", None, None), P(), P(), P("mode"))
    out_specs = P("sector", "mode")
    return jax.shard_map(
        on_device, mesh=mesh, in_specs=in_specs, out_specs=out_specs, check_vma=False
    )
```
